32 devices in a mesh: row: 4 (over y, x), col: 8 (over z, core).
Axes of the slice: x: 2, y: 2, z: 4, core: 2. Of those that a mesh axis runs over, the one named last changes fastest.
Arguments:
- g_first: float32 [1024, 2048], P('col'), may hold values from -6 to 6
- g_second: float32 [1024, 2048], P('col'), may hold values from -6 to 6
- y_head: float32 [63488, 2048], P(('row', 'col')), may hold values from -6 to 6
- l_rows: float32 [2048, 63488], P(None, ('row', 'col')), may hold values from -0.125 to 0.125
- ut_first_inv: float32 [1024, 1024], P('row', 'col'), as said below
- ut_cross: float32 [1024, 1024], P('col', 'row'), may hold values from -0.09375 to 0.09375
- ut_second_inv: float32 [1024, 1024], P('row', 'col'), as said below
- lt_second_inv: float32 [1024, 1024], P('col', 'row'), as said below
- lt_cross: float32 [1024, 1024], P('row', 'col'), may hold values from -0.09375 to 0.09375
- lt_first_inv: float32 [1024, 1024], P('col', 'row'), as said below
Outputs:
- x_first: float32 [1024, 2048], P('col', 'row')
- x_second: float32 [1024, 2048], P('col', 'row')
- head_out: float32 [63488, 2048], P(('row', 'col'))
The draws below stay inside these ranges and needn't reach their ends.
Inputs may be any that keep to these rules, and one draw needn't show every extreme that they name: `ut_first_inv`: lower triangular with a positive diagonal. `ut_second_inv`: lower triangular with a positive diagonal. `lt_second_inv`: upper triangular with a unit diagonal. `lt_first_inv`: upper triangular with a unit diagonal.
All inputs are finite; a program needn't handle non-finite values.
Results may differ from the reference program's by a relative error of at most 0.000084.
Values sent between devices are 32-bit elements; how exact they have to be, the bound alone decides.
A program may use at most 192 MiB of HBM per device.

```python
import math
import jax
import jax.numpy as jnp
from jax import lax

P_SIZE = 1024
R = 2048
H = 63488


def triangle(key, lower, unit):
    first_key, second_key = jax.random.split(key)
    noise = jax.random.normal(first_key, (P_SIZE, P_SIZE), jnp.float32) * (0.5 / math.sqrt(P_SIZE))
    rows = jnp.arange(P_SIZE)[:, None]
    cols = jnp.arange(P_SIZE)[None, :]
    if lower:
        keep = rows > cols
    else:
        keep = rows < cols
    if unit:
        diagonal = jnp.ones((P_SIZE,), jnp.float32)
    else:
        diagonal = jnp.exp(jax.random.uniform(second_key, (P_SIZE,), jnp.float32, -math.log(2.0), math.log(2.0)))
    return jnp.where(keep, noise, 0.0) + jnp.diag(diagonal)


def draw_ut_first_inv(key, part):
    key = jax.random.fold_in(key, 3)
    return triangle(key, True, False)


def draw_ut_second_inv(key, part):
    key = jax.random.fold_in(key, 5)
    return triangle(key, True, False)


def draw_lt_second_inv(key, part):
    key = jax.random.fold_in(key, 7)
    return triangle(key, False, True)


def draw_lt_first_inv(key, part):
    key = jax.random.fold_in(key, 11)
    return triangle(key, False, True)


def levels(stream_key, shape, pieces, smallest, largest):
    level, own = 1.0, jax.random.fold_in(stream_key, 6)
    for dim, shards_of in pieces:
        heights = jnp.exp(jax.random.uniform(jax.random.fold_in(own, dim), (shards_of,), jnp.float32, smallest / len(pieces), largest / len(pieces)))
        level = level * jnp.repeat(heights, shape[dim] // shards_of).reshape([-1 if axis == dim else 1 for axis in range(len(shape))])
    return level


def gaussian(own_key, dims, deviation, bound, shards=(), held_as=jnp.bfloat16):
    factor_of = levels(own_key, dims, shards, -0.22, 0.18) if shards else 1.0
    entries = jax.random.normal(own_key, dims, jnp.float32) * deviation * factor_of
    return jnp.minimum(jnp.maximum(entries, -bound), bound).astype(held_as)


def setup_inputs(seed: int = 0) -> dict:
    splits = jax.random.split(jax.random.key(seed), 11)
    g_first = gaussian(splits[0], (P_SIZE, R), 1.0, 6.0, ((0, 8),), jnp.float32)
    g_second = gaussian(splits[1], (P_SIZE, R), 1.0, 6.0, ((0, 8),), jnp.float32)
    y_head = gaussian(splits[2], (H, R), 1.0, 6.0, ((0, 32),), jnp.float32)
    l_rows = gaussian(splits[3], (2 * P_SIZE, H), (2 * P_SIZE) ** -0.5, 0.125, ((1, 32),), jnp.float32)
    ut_first_inv = draw_ut_first_inv(jax.random.fold_in(splits[10], 71), 0)
    ut_cross = gaussian(splits[5], (P_SIZE, P_SIZE), (4 * P_SIZE) ** -0.5, 0.09375, ((0, 8), (1, 4)), jnp.float32)
    ut_second_inv = draw_ut_second_inv(jax.random.fold_in(splits[10], 71), 0)
    lt_second_inv = draw_lt_second_inv(jax.random.fold_in(splits[10], 71), 0)
    lt_cross = gaussian(splits[8], (P_SIZE, P_SIZE), (4 * P_SIZE) ** -0.5, 0.09375, ((0, 4), (1, 8)), jnp.float32)
    lt_first_inv = draw_lt_first_inv(jax.random.fold_in(splits[10], 71), 0)
    return dict(g_first=g_first, g_second=g_second, y_head=y_head, l_rows=l_rows, ut_first_inv=ut_first_inv, ut_cross=ut_cross, ut_second_inv=ut_second_inv, lt_second_inv=lt_second_inv, lt_cross=lt_cross, lt_first_inv=lt_first_inv)


def product(left, right):
    return jnp.dot(left, right, precision=lax.Precision.HIGHEST, preferred_element_type=jnp.float32)


def reference(g_first, g_second, y_head, l_rows, ut_first_inv, ut_cross, ut_second_inv, lt_second_inv, lt_cross, lt_first_inv):
    y_first = product(ut_first_inv, g_first)
    y_second = product(ut_second_inv, g_second - product(ut_cross, y_first))
    x_second = product(lt_second_inv, y_second)
    x_first = product(lt_first_inv, y_first - product(lt_cross, x_second))
    stacked = jnp.concatenate([x_first, x_second], axis=0)
    update = lax.dot_general(l_rows, stacked, (((0,), (0,)), ((), ())), precision=lax.Precision.HIGHEST, preferred_element_type=jnp.float32)
    head_out = y_head - update
    return x_first, x_second, head_out
```

```python
import jax
import jax.numpy as jnp
from jax import lax
from jax.sharding import PartitionSpec as P

BOTH = ("row", "col")


def times(left, right, left_dim, right_dim):
    return lax.dot_general(
        left,
        right,
        (((left_dim,), (right_dim,)), ((), ())),
        precision=lax.Precision.HIGH,
        preferred_element_type=jnp.float32,
    )


def shards(
    g_first,
    g_second,
    y_head,
    l_rows,
    ut_first_inv,
    ut_cross,
    ut_second_inv,
    lt_second_inv,
    lt_cross,
    lt_first_inv,
):
    panel = l_rows.shape[0] // 2
    rows, cols = lax.axis_size("row"), lax.axis_size("col")
    row, col = lax.axis_index("row"), lax.axis_index("col")
    width = g_first.shape[1] // rows
    depth = g_first.shape[0]

    def own_columns(g):
        return lax.dynamic_slice_in_dim(g, row * width, width, 1).T

    g = jnp.stack([own_columns(g_first), own_columns(g_second)], axis=1)
    g = lax.all_to_all(g, "col", 0, 2, tiled=True)

    def gather_pair(by_row, by_col):
        blocks = lax.all_gather(jnp.stack([by_row, by_col.T]), BOTH)
        tall, wide = by_row.shape
        blocks = blocks.reshape(rows, cols, 2, tall, wide).transpose(2, 0, 3, 1, 4)
        return blocks.reshape(2, panel, panel)

    first_pair = gather_pair(ut_first_inv, ut_cross)
    second_pair = gather_pair(ut_second_inv, lt_second_inv)
    third_pair = gather_pair(lt_cross, lt_first_inv)

    y_first = times(g[:, 0], first_pair[0], 1, 1)
    shifted = g[:, 1] - times(y_first, first_pair[1], 1, 0)
    y_second = times(shifted, second_pair[0], 1, 1)
    x_second = times(y_second, second_pair[1], 1, 0)
    second_all = lax.all_gather(x_second, BOTH, axis=0, tiled=True)
    corrected = y_first - times(x_second, third_pair[0], 1, 1)
    x_first = times(corrected, third_pair[1], 1, 0)
    first_all = lax.all_gather(x_first, BOTH, axis=0, tiled=True)

    head = y_head - times(l_rows[panel:], second_all, 0, 1)
    head = head - times(l_rows[:panel], first_all, 0, 1)

    def own_block(x):
        return lax.dynamic_slice(x, (row * width, col * depth), (width, depth)).T

    return (own_block(first_all), own_block(second_all), head)


def solution(mesh):
    return jax.shard_map(
        shards,
        mesh=mesh,
        in_specs=(
            P("col", None),
            P("col", None),
            P(("row", "col"), None),
            P(None, ("row", "col")),
            P("row", "col"),
            P("col", "row"),
            P("row", "col"),
            P("col", "row"),
            P("row", "col"),
            P("col", "row"),
        ),
        out_specs=(P("col", "row"), P("col", "row"), P(("row", "col"), None)),
        check_vma=False,
    )
```

```python
import jax
import jax.numpy as jnp
from jax import lax
from jax.sharding import Mesh, PartitionSpec as P

CHIPS = ("row", "z")
COL = ("z", "core")


def times(left, right, left_dim, right_dim):
    return lax.dot_general(
        left,
        right,
        (((left_dim,), (right_dim,)), ((), ())),
        precision=lax.Precision.HIGH,
        preferred_element_type=jnp.float32,
    )


def shards(
    g_first,
    g_second,
    y_head,
    l_rows,
    ut_first_inv,
    ut_cross,
    ut_second_inv,
    lt_second_inv,
    lt_cross,
    lt_first_inv,
):
    panel = l_rows.shape[0] // 2
    rows, zs, cores = (lax.axis_size(axis) for axis in ("row", "z", "core"))
    row = lax.axis_index("row")
    col = lax.axis_index("z") * cores + lax.axis_index("core")
    depth, total = g_first.shape
    width = total // rows

    def own_columns(g):
        parts = g.T.reshape(cores, rows, zs, width // (zs * cores), depth)
        parts = lax.dynamic_index_in_dim(parts, row, 1, keepdims=False)
        return parts.transpose(1, 0, 2, 3).reshape(width, depth)

    def swap_blocks(x, outer, inner):
        pieces = jnp.split(x, outer * inner, axis=-1)
        order = [a * inner + b for b in range(inner) for a in range(outer)]
        return jnp.concatenate([pieces[place] for place in order], axis=-1)

    g = jnp.stack([own_columns(g_first), own_columns(g_second)], axis=1)
    g = lax.all_to_all(g, COL, 0, 2, tiled=True)
    g = swap_blocks(g, zs, cores)

    def spread(x, chips=CHIPS):
        across = lax.all_gather(x, chips, axis=0, tiled=True)
        return lax.all_gather(across, "core", axis=0, tiled=True)

    def gather_pair(by_row, by_col):
        return spread(jnp.stack([by_row, by_col.T])[None], CHIPS[::-1])

    def arrange(blocks):
        tall, wide = blocks.shape[2:]
        blocks = blocks.reshape(cores * zs, rows, 2, tall, wide).transpose(2, 1, 3, 0, 4)
        return blocks.reshape(2, panel, panel)

    first_pair = arrange(gather_pair(ut_first_inv, ut_cross))
    second_pair = arrange(gather_pair(ut_second_inv, lt_second_inv))
    third_blocks = gather_pair(lt_cross, lt_first_inv)

    y_first = times(g[:, 0], first_pair[0], 1, 1)
    shifted = g[:, 1] - times(y_first, first_pair[1], 1, 0)
    y_second = times(shifted, second_pair[0], 1, 1)
    x_second = times(y_second, second_pair[1], 1, 0)
    x_second, third_blocks = lax.optimization_barrier((x_second, third_blocks))
    third_pair = arrange(third_blocks)
    second_all = spread(swap_blocks(x_second, cores, zs))
    corrected = y_first - times(x_second, third_pair[0], 1, 1)
    x_first = times(corrected, third_pair[1], 1, 0)
    x_first, second_all = lax.optimization_barrier((x_first, second_all))
    first_all = spread(swap_blocks(x_first, cores, zs))

    head = y_head - times(l_rows[panel:], second_all, 0, 1)
    head = head - times(l_rows[:panel], first_all, 0, 1)

    def own_block(x):
        return lax.dynamic_slice(x, (row * width, col * depth), (width, depth)).T

    return (own_block(first_all), own_block(second_all), head)


def solution(mesh):
    rows, cols = mesh.devices.shape
    split = Mesh(mesh.devices.reshape(rows, cols // 2, 2), ("row", "z", "core"))
    by_col, by_both = P(COL, None), P(("row",) + COL, None)
    return jax.shard_map(
        shards,
        mesh=split,
        in_specs=(
            by_col,
            by_col,
            by_both,
            P(None, ("row",) + COL),
            P("row", COL),
            P(COL, "row"),
            P("row", COL),
            P(COL, "row"),
            P("row", COL),
            P(COL, "row"),
        ),
        out_specs=(P(COL, "row"), P(COL, "row"), by_both),
        check_vma=False,
    )
```

```python
import jax
import jax.numpy as jnp
from jax import lax
from jax.sharding import PartitionSpec as P

BOTH = ("row", "col")


def times(left, right, left_dim, right_dim):
    return lax.dot_general(
        left,
        right,
        (((left_dim,), (right_dim,)), ((), ())),
        precision=lax.Precision.HIGH,
        preferred_element_type=jnp.float32,
    )


def shards(
    g_first,
    g_second,
    y_head,
    l_rows,
    ut_first_inv,
    ut_cross,
    ut_second_inv,
    lt_second_inv,
    lt_cross,
    lt_first_inv,
):
    panel = l_rows.shape[0] // 2
    rows, cols = lax.axis_size("row"), lax.axis_size("col")
    row, col = lax.axis_index("row"), lax.axis_index("col")
    width = g_first.shape[1] // rows
    depth = g_first.shape[0]

    def own_columns(g):
        return lax.dynamic_slice_in_dim(g, row * width, width, 1).T

    g = jnp.stack([own_columns(g_first), own_columns(g_second)], axis=1)
    g = lax.all_to_all(g, "col", 0, 2, tiled=True)

    def gather_pair(by_row, by_col):
        return lax.all_gather(jnp.stack([by_row, by_col.T]), BOTH)

    def arrange(blocks):
        tall, wide = blocks.shape[2:]
        blocks = blocks.reshape(rows, cols, 2, tall, wide).transpose(2, 0, 3, 1, 4)
        return blocks.reshape(2, panel, panel)

    first_pair = arrange(gather_pair(ut_first_inv, ut_cross))
    second_pair = arrange(gather_pair(ut_second_inv, lt_second_inv))
    third_blocks = gather_pair(lt_cross, lt_first_inv)

    y_first = times(g[:, 0], first_pair[0], 1, 1)
    shifted = g[:, 1] - times(y_first, first_pair[1], 1, 0)
    y_second = times(shifted, second_pair[0], 1, 1)
    x_second = times(y_second, second_pair[1], 1, 0)
    x_second, third_blocks = lax.optimization_barrier((x_second, third_blocks))
    third_pair = arrange(third_blocks)
    second_all = lax.all_gather(x_second, BOTH, axis=0, tiled=True)
    corrected = y_first - times(x_second, third_pair[0], 1, 1)
    x_first = times(corrected, third_pair[1], 1, 0)
    x_first, second_all = lax.optimization_barrier((x_first, second_all))
    first_all = lax.all_gather(x_first, BOTH, axis=0, tiled=True)

    head = y_head - times(l_rows[panel:], second_all, 0, 1)
    head = head - times(l_rows[:panel], first_all, 0, 1)

    def own_block(x):
        return lax.dynamic_slice(x, (row * width, col * depth), (width, depth)).T

    return (own_block(first_all), own_block(second_all), head)


def solution(mesh):
    return jax.shard_map(
        shards,
        mesh=mesh,
        in_specs=(
            P("col", None),
            P("col", None),
            P(("row", "col"), None),
            P(None, ("row", "col")),
            P("row", "col"),
            P("col", "row"),
            P("row", "col"),
            P("col", "row"),
            P("row", "col"),
            P("col", "row"),
        ),
        out_specs=(P("col", "row"), P("col", "row"), P(("row", "col"), None)),
        check_vma=False,
    )
```
